32 devices in a mesh: row: 8 (over z, x), col: 4 (over y, core).
Axes of the slice: x: 2, y: 2, z: 4, core: 2. Of those that a mesh axis runs over, the one named last changes fastest.
Arguments:
- hamiltonian: bfloat16 [16, 4, 2, 2, 128, 128], P('row', 'col'), may hold values from -0.14142136 to 0.14142136, as said below
- density: float32 [16, 4, 2, 2, 128, 128], P('row', 'col'), may hold values from -6.4 to 6.4, as said below
- block_cols: int32 [16, 4, 2], P('row', 'col'), may hold values from 0 to 15, as said below
Outputs:
- commutator: float32 [16, 4, 2, 2, 128, 128], P('row', 'col')
- density_section: float32 [16, 4, 2, 2, 128, 128], P('row', 'col')
The draws below stay inside these ranges and needn't reach their ends.
Inputs may be any that keep to these rules, and one draw needn't show every extreme that they name: `block_cols`: block rows 2 d to 2 d + 1 lie on device d along row. A permutation drawn for each device gives each of its block rows a fiber f from 0 to 1, each fiber once a device. With P the number of devices along col and t = (c - d) mod P, slot (c, 0) of a block row of fiber f on device d holds the block row of fiber f on device (d + t) mod (8); slot (c, 1) holds, for t > 0, the block row of fiber f on device (d + t - P) mod (8), and for t = 0 the block row of fiber f + 1 - 2 (f mod 2) on device d. So the pattern is symmetric and every slot (i, j) lies in column group (j div 2) mod P. `hamiltonian`: Hermitian: the block of row i for column j is the conjugate transpose of the block of row j for column i. `density`: Hermitian: the block of row i for column j is the conjugate transpose of the block of row j for column i.
All inputs are finite; a program needn't handle non-finite values.
Results may differ from the reference program's by a relative error of at most 0.0029.
Values may be sent and summed in bfloat16 or wider, within the bound.
No kernel may reach another device: no remote copies, remote signals or barrier semaphores. Data moves between devices by JAX's collectives and lax.ppermute only.
A program may use at most 64 MiB of HBM per device.

```python
import jax
import jax.numpy as jnp
from jax import lax

BS = 128
KC = 2
RB = 2
NB = 16
N_COL = 4


def pattern_cols(key):
    device_total = NB // RB
    device_keys = jax.random.split(key, device_total)
    fibers = jax.vmap(lambda one_key: jax.random.permutation(one_key, RB))(device_keys).astype(jnp.int32)
    inverse = jnp.argsort(fibers, axis=1).astype(jnp.int32)
    device_ids = jnp.arange(device_total, dtype=jnp.int32)[:, None, None, None]
    local_rows = jnp.arange(RB, dtype=jnp.int32)[None, :, None, None]
    groups = jnp.arange(N_COL, dtype=jnp.int32)[None, None, :, None]
    halves = jnp.arange(KC, dtype=jnp.int32)[None, None, None, :]
    residue = (groups - device_ids) % N_COL
    offset = jnp.where(halves == 0, residue, jnp.where(residue == 0, 0, residue - N_COL))
    target = (device_ids + offset) % device_total
    fiber_own = inverse[device_ids, local_rows]
    partner = fiber_own + 1 - 2 * (fiber_own % 2)
    target_fiber = jnp.where((halves == 1) & (residue == 0), partner, fiber_own)
    full_shape = (device_total, RB, N_COL, KC)
    target_full = jnp.broadcast_to(target, full_shape)
    fiber_full = jnp.broadcast_to(target_fiber, full_shape)
    column = RB * target_full + fibers[target_full, fiber_full]
    return column.reshape(NB, N_COL, KC).astype(jnp.int32)


def hermitian_blocks(key, salt, spread):
    slot_count = N_COL * KC
    pattern = pattern_cols(jax.random.fold_in(key, 7)).reshape(NB, slot_count)
    shape = (NB * slot_count, 2, BS, BS)
    value_key = jax.random.fold_in(jax.random.fold_in(key, salt), 29)
    drawn = jnp.clip(jax.random.normal(value_key, shape, jnp.float32), -4.5, 4.5)
    returned_cols = pattern[pattern]
    matches = returned_cols == jnp.arange(NB, dtype=jnp.int32)[:, None, None]
    mirror_slot = jnp.sum(jnp.where(matches, jnp.arange(slot_count, dtype=jnp.int32)[None, None, :], 0), axis=2).astype(jnp.int32)
    flat_index = (pattern * slot_count + mirror_slot).reshape(-1).astype(jnp.int32)
    mirrored = drawn[flat_index]
    adjoint = jnp.stack([jnp.swapaxes(mirrored[:, 0], -1, -2), -jnp.swapaxes(mirrored[:, 1], -1, -2)], axis=1)
    blocks = (drawn + adjoint) * (spread / 1.4142135)
    return blocks.reshape(NB, N_COL, KC, 2, BS, BS)


def draw_block_cols(key, part):
    return pattern_cols(jax.random.fold_in(key, 7))


def draw_hamiltonian(key, part):
    spread = (4.0 * N_COL * BS) ** (-0.5)
    return hermitian_blocks(key, 11, spread).astype(jnp.bfloat16)


def draw_density(key, part):
    return hermitian_blocks(key, 13, 1.0).astype(jnp.float32)


def setup_inputs(seed: int = 0) -> dict:
    seeds = jax.random.split(jax.random.key(seed), 4)
    return {
        "hamiltonian": draw_hamiltonian(jax.random.fold_in(seeds[3], 71), 0),
        "density": draw_density(jax.random.fold_in(seeds[3], 71), 0),
        "block_cols": draw_block_cols(jax.random.fold_in(seeds[3], 71), 0),
    }


def complex_sum(left_side, right_side):
    real_part = jnp.einsum('sab,sckbd->ckad', left_side[:, 0], right_side[:, :, :, 0]) - jnp.einsum('sab,sckbd->ckad', left_side[:, 1], right_side[:, :, :, 1])
    imag_part = jnp.einsum('sab,sckbd->ckad', left_side[:, 0], right_side[:, :, :, 1]) + jnp.einsum('sab,sckbd->ckad', left_side[:, 1], right_side[:, :, :, 0])
    return jnp.stack([real_part, imag_part], axis=2)


def mirror_blocks(blocks, block_cols):
    slot_count = N_COL * KC
    flat_cols = block_cols.reshape(NB, slot_count)
    returned_cols = flat_cols[flat_cols]
    matches = returned_cols == jnp.arange(NB, dtype=jnp.int32)[:, None, None]
    mirror_slot = jnp.sum(jnp.where(matches, jnp.arange(slot_count, dtype=jnp.int32)[None, None, :], 0), axis=2).astype(jnp.int32)
    flat_index = (flat_cols * slot_count + mirror_slot).reshape(-1).astype(jnp.int32)
    mirrored = blocks.reshape(NB * slot_count, 2, BS, BS)[flat_index]
    adjoint = jnp.stack([jnp.swapaxes(mirrored[:, 0], -1, -2), -jnp.swapaxes(mirrored[:, 1], -1, -2)], axis=1)
    return adjoint.reshape(blocks.shape)


def reference(hamiltonian, density, block_cols):
    slot_count = N_COL * KC
    flat_cols = block_cols.reshape(NB, slot_count)
    density_half = density.astype(jnp.bfloat16)

    def one_row(row_index):
        neighbors = flat_cols[row_index]
        wanted = block_cols[row_index]
        nearby_cols = block_cols[neighbors]
        matches = (nearby_cols[:, :, None, :] == wanted[None, :, :, None]).astype(jnp.float32)
        nearby_state = density_half[neighbors].astype(jnp.float32)
        state_match = jnp.einsum('scmn,scnxab->scmxab', matches, nearby_state)
        own_energy = hamiltonian[row_index].reshape(slot_count, 2, BS, BS).astype(jnp.float32)
        return complex_sum(own_energy, state_match)

    product = lax.map(one_row, jnp.arange(NB, dtype=jnp.int32))
    reverse = mirror_blocks(product, block_cols)
    commutator = product - reverse
    turned = jnp.stack([commutator[:, :, :, 1], -commutator[:, :, :, 0]], axis=3)
    density_section = density + 0.05 * turned
    return commutator, density_section
```

```python
import functools

import jax
import jax.numpy as jnp
from jax import lax
from jax.experimental import pallas as pl
from jax.experimental.pallas import tpu as pltpu
from jax.sharding import PartitionSpec as P


REACH = 3


def xor_col(value, group_count, by):
    return lax.ppermute(value, "col", [(i, i ^ by) for i in range(group_count)])


def sign_of(col):
    return 1 - 2 * (col % 2)


def row_pairs(row_count, group_count, step):
    pairs = []
    for row in range(row_count):
        for col in range(group_count):
            target = (row + step * sign_of(col)) % row_count
            pairs.append((row * group_count + col, target * group_count + col))
    return pairs


def slot_stack(ref, row, slot):
    return ref[row, slot]


def fill_right(right, row, place, stack, size):
    energy_re = stack[0 * size:1 * size]
    energy_im = stack[1 * size:2 * size]
    state_re = stack[2 * size:3 * size]
    state_im = stack[3 * size:4 * size]
    left = pl.ds(2 * place * size, size)
    here = pl.ds((2 * place + 1) * size, size)
    right[row, 0 * size:1 * size, left] = state_re
    right[row, 0 * size:1 * size, here] = state_im
    right[row, 1 * size:2 * size, left] = state_im
    right[row, 1 * size:2 * size, here] = -state_re
    right[row, 2 * size:3 * size, left] = -energy_re
    right[row, 2 * size:3 * size, here] = -energy_im
    right[row, 3 * size:4 * size, left] = -energy_im
    right[row, 3 * size:4 * size, here] = energy_re


def times(left, right):
    return lax.dot_general(
        left, right, (((0,), (0,)), ((), ())), preferred_element_type=jnp.float32
    )


def chosen(index, values):
    out = values[0]
    for place in range(1, len(values)):
        out = jnp.where(index == place, values[place], out)
    return out


def terms_kernel(shape, own_cols, near_cols, *refs):
    row_count, group_count, rows, slots, size = shape
    stacks = refs[:group_count]
    outs = refs[group_count:group_count + REACH]
    right = refs[group_count + REACH]
    me = lax.axis_index("row")
    col = lax.axis_index("col")
    cols = (own_cols, near_cols)
    for row in range(rows):
        for pair in range(2):
            for slot in range(slots):
                fill_right(right, row, pair * slots + slot, slot_stack(stacks[pair], row, slot), size)
    sign = 1 - 2 * (col % 2)
    for step in range(1, REACH + 1):
        offset = step * sign
        target = (me + offset + row_count) % row_count
        held = (target % group_count) ^ col
        held_slot = jnp.where(offset > 0, 0, 1)
        for row in range(rows):
            left = chosen(held, [ref[row, held_slot] for ref in stacks])
            full = times(left, right[row])
            for pair in range(2):
                pair_col = col ^ pair
                mine = (pair_col - me + row_count) % group_count
                theirs = (pair_col - target + row_count) % group_count
                for slot in range(slots):
                    shift = offset + theirs - group_count * slot - mine + 2 * row_count
                    first = shift % row_count == 0
                    second = ((shift + group_count) % row_count == 0) & (mine != 0)
                    wanted = jnp.logical_or(slot == 0, theirs != 0)
                    valid = wanted & (first | second)
                    begin = 2 * pair * slots * size
                    part = jnp.where(
                        second,
                        full[:, begin + 2 * size:begin + 4 * size],
                        full[:, begin:begin + 2 * size],
                    )
                    part = jnp.where(valid, part, 0.0).astype(jnp.bfloat16)
                    place = jnp.where(second, cols[pair][row, 1], cols[pair][row, 0]) % rows
                    place = jnp.where(valid, place, row)
                    outs[step - 1][pair, slot, place, 0] = part[:, :size]
                    outs[step - 1][pair, slot, place, 1] = part[:, size:]


def own_kernel(shape, own_cols, *refs):
    row_count, group_count, rows, slots, size = shape
    stacks = refs[:group_count]
    out = refs[group_count]
    right = refs[group_count + 1]
    me = lax.axis_index("row")
    col = lax.axis_index("col")
    for row in range(rows):
        for slot in range(slots):
            fill_right(right, row, slot, slot_stack(stacks[0], row, slot), size)
    held = (me % group_count) ^ col
    for row in range(rows):
        left = chosen(held, [ref[row, 0] for ref in stacks])
        full = times(left, right[row])
        for slot in range(slots):
            out[row, slot, 0] = full[:, 2 * slot * size:(2 * slot + 1) * size]
            out[row, slot, 1] = full[:, (2 * slot + 1) * size:(2 * slot + 2) * size]

    @pl.when(held == 0)
    def _():
        for row in range(rows):
            partner = own_cols[row, 1] % rows
            full = times(stacks[0][partner, 1], right[partner])
            for slot in range(slots):
                begin = 2 * (1 - slot) * size
                out[row, slot, 0] += full[:, begin:begin + size]
                out[row, slot, 1] += full[:, begin + size:begin + 2 * size]


def finish_kernel(count, cols, *refs):
    own = refs[0]
    density = refs[1]
    commutator = refs[2 + count]
    section = refs[3 + count]
    real = own[0, 0, 0]
    imag = own[0, 0, 1]
    for ref in refs[2:2 + count]:
        real += ref[0, 0, 0, 0].astype(jnp.float32)
        imag += ref[0, 0, 0, 1].astype(jnp.float32)
    commutator[0, 0, 0, 0] = real
    commutator[0, 0, 0, 1] = imag
    section[0, 0, 0, 0] = density[0, 0, 0, 0] + 0.05 * imag
    section[0, 0, 0, 1] = density[0, 0, 0, 1] - 0.05 * real


def body(hamiltonian, density, block_cols):
    row_count = lax.axis_size("row")
    group_count = lax.axis_size("col")
    rows, _, slots, parts, size, _ = hamiltonian.shape
    shape = (row_count, group_count, rows, slots, size)
    smem = pl.BlockSpec(memory_space=pltpu.SMEM)
    vmem = pl.BlockSpec(memory_space=pltpu.VMEM)
    params = pltpu.CompilerParams(vmem_limit_bytes=40 * 1024 * 1024)

    own_cols = block_cols[:, 0]
    stack = jnp.stack([hamiltonian[:, 0], density[:, 0].astype(jnp.bfloat16)], axis=2)
    stack = stack.reshape(rows, slots, 2 * parts * size, size)
    stacks = [stack]
    for by in range(1, group_count):
        if by % 2 == 0:
            stacks.append(xor_col(stack, group_count, by))
        else:
            stacks.append(xor_col(stacks[by - 1], group_count, 1))
    near_cols = xor_col(own_cols, group_count, 1)

    message = jax.ShapeDtypeStruct((2, slots, rows, parts, size, size), jnp.bfloat16)
    sent = pl.pallas_call(
        functools.partial(terms_kernel, shape),
        out_shape=[message] * REACH,
        in_specs=[smem, smem] + [vmem] * group_count,
        out_specs=[vmem] * REACH,
        scratch_shapes=[pltpu.VMEM((rows, 4 * size, 4 * slots * size), jnp.bfloat16)],
        compiler_params=params,
        name="terms",
    )(own_cols, near_cols, *stacks)
    own = pl.pallas_call(
        functools.partial(own_kernel, shape),
        out_shape=jax.ShapeDtypeStruct((rows, slots, parts, size, size), jnp.float32),
        in_specs=[smem] + [vmem] * group_count,
        out_specs=vmem,
        scratch_shapes=[pltpu.VMEM((rows, 4 * size, 2 * slots * size), jnp.bfloat16)],
        compiler_params=params,
        name="own_terms",
    )(own_cols, *stacks)

    arrived = []
    for step in range(1, REACH + 1):
        pairs = row_pairs(row_count, group_count, step)
        arrived.append(lax.ppermute(sent[step - 1], ("row", "col"), pairs))
    swapped = [xor_col(one[1:], group_count, 1) for one in arrived]
    terms = arrived + swapped

    flat_cols = own_cols.reshape(-1)
    block = (1, 1, 1, parts, size, size)

    def term_index(row, slot, cols):
        return (0, slot, cols[row * slots + slot] % rows, 0, 0, 0)

    def slot_index(row, slot, cols):
        return (row, slot, 0, 0, 0)

    def home_index(row, slot, cols):
        return (row, 0, slot, 0, 0, 0)

    commutator, section = pl.pallas_call(
        functools.partial(finish_kernel, len(terms)),
        out_shape=[jax.ShapeDtypeStruct(density.shape, jnp.float32)] * 2,
        grid_spec=pltpu.PrefetchScalarGridSpec(
            num_scalar_prefetch=1,
            grid=(rows, slots),
            in_specs=[
                pl.BlockSpec((1, 1, parts, size, size), slot_index),
                pl.BlockSpec(block, home_index),
            ] + [pl.BlockSpec(block, term_index)] * len(terms),
            out_specs=[pl.BlockSpec(block, home_index)] * 2,
        ),
        compiler_params=params,
        name="finish",
    )(flat_cols, own, density, *terms)
    return commutator, section


def solution(mesh):
    blocks = P("row", "col", None, None, None, None)
    return jax.shard_map(
        body,
        mesh=mesh,
        in_specs=(blocks, blocks, P("row", "col", None)),
        out_specs=(blocks, blocks),
        check_vma=False,
    )
```

```python
import functools

import jax
import jax.numpy as jnp
import numpy as np
from jax import lax
from jax.experimental import pallas as pl
from jax.experimental.pallas import tpu as pltpu
from jax.sharding import PartitionSpec as P


SLOTS = 2
PAIR = 2


def xor_col(value, group_count, by):
    return lax.ppermute(value, "col", [(i, i ^ by) for i in range(group_count)])


class Plan:
    def __init__(self, row_count, group_count):
        assert group_count == 4
        self.turns = [0, 1, 2]
        self.pairs = {turn: [] for turn in self.turns}
        self.width = {turn: 0 for turn in self.turns}
        sends = {}
        finds = {}
        for row in range(row_count):
            for first in range(0, group_count, PAIR):
                for offset in range(1 - group_count, group_count):
                    if offset == 0:
                        continue
                    target = (row + offset) % row_count
                    turn, sender, side = self.way(row, first, offset, target, group_count)
                    taker = first + side
                    blocks = self.blocks(row, first, target, row_count, group_count)
                    codes = []
                    for column, slot, have in blocks:
                        place = (target, column, slot, turn, taker ^ column)
                        assert place not in finds
                        finds[place] = len(codes)
                        codes.append((column ^ sender) * SLOTS + have)
                    held = ((target % group_count) ^ sender) * SLOTS + (0 if offset > 0 else 1)
                    assert (row, sender, turn) not in sends
                    sends[row, sender, turn] = (held, codes)
                    self.pairs[turn].append(
                        (row * group_count + sender, target * group_count + taker)
                    )
                    self.width[turn] = max(self.width[turn], len(codes))
        lines = []
        for row in range(row_count):
            for col in range(group_count):
                line = []
                self.send_at = {}
                for turn in self.turns:
                    held, codes = sends.get((row, col, turn), (-1, []))
                    self.send_at[turn] = len(line)
                    line += [held] + codes + [-1] * (self.width[turn] - len(codes))
                self.find_at = {}
                for turn in self.turns:
                    for pair in range(PAIR):
                        self.find_at[turn, pair] = len(line)
                        line += [finds.get((row, col, slot, turn, pair), -1) for slot in range(SLOTS)]
                lines.append(line)
        self.table = np.asarray(lines, np.int32)

    def way(self, row, first, offset, target, group_count):
        if (target % group_count) // PAIR == (row % group_count) // PAIR:
            return 2, first + (target + (offset > 0)) % PAIR, int(offset > 0)
        turn = int(offset == -2 or abs(offset) == 3)
        return turn, first + target % PAIR, int(abs(offset) == 2)

    def blocks(self, row, first, target, row_count, group_count):
        found = []
        for column in range(first, first + PAIR):
            mine = (column - row) % group_count
            theirs = (column - target) % group_count
            have = {(row + mine) % row_count: 0}
            if mine:
                have[(row + mine - group_count) % row_count] = 1
            for slot in range(SLOTS if theirs else 1):
                wanted = (target + theirs - group_count * slot) % row_count
                if wanted in have:
                    found.append((column, slot, have[wanted]))
        return found


def fill_right(right, row, place, stack, size):
    energy_re = stack[0 * size:1 * size]
    energy_im = stack[1 * size:2 * size]
    state_re = stack[2 * size:3 * size]
    state_im = stack[3 * size:4 * size]
    right[row, place, 0 * size:1 * size, :size] = state_re
    right[row, place, 0 * size:1 * size, size:] = state_im
    right[row, place, 1 * size:2 * size, :size] = state_im
    right[row, place, 1 * size:2 * size, size:] = -state_re
    right[row, place, 2 * size:3 * size, :size] = -energy_re
    right[row, place, 2 * size:3 * size, size:] = -energy_im
    right[row, place, 3 * size:4 * size, :size] = -energy_im
    right[row, place, 3 * size:4 * size, size:] = energy_re


def times(left, right):
    return lax.dot_general(
        left, right, (((0,), (0,)), ((), ())), preferred_element_type=jnp.float32
    )


def chosen(index, values):
    out = values[0]
    for place in range(1, len(values)):
        out = jnp.where(index == place, values[place], out)
    return out


def terms_kernel(plan, turns, group_count, rows, size, line, own_cols, near_cols, *refs):
    stacks = refs[:-len(turns) - 2]
    outs = refs[-len(turns) - 2:-2]
    own, right = refs[-2:]
    for row in range(rows):
        for pair in range(PAIR):
            for slot in range(SLOTS):
                fill_right(right, row, pair * SLOTS + slot, stacks[pair][row, slot], size)
    for turn, out in zip(turns, outs):
        base = plan.send_at[turn]
        held = line[base]
        for row in range(rows):
            values = [ref[row, held % SLOTS] for ref in stacks[:PAIR + 1]]
            values += [ref[row] for ref in stacks[PAIR + 1:]]
            left = chosen(held // SLOTS, values)
            for place in range(plan.width[turn]):
                code = jnp.maximum(line[base + 1 + place], 0)
                pair = code // SLOTS
                slot = code % SLOTS
                full = times(left, right[row, code]).astype(jnp.bfloat16)
                there = jnp.where(pair == 0, own_cols[row, slot], near_cols[row, slot]) % rows
                out[place, there, 0] = full[:, :size]
                out[place, there, 1] = full[:, size:]
    if len(stacks) == group_count:
        own_part(group_count, rows, size, own_cols, stacks, right, own)


def own_part(group_count, rows, size, own_cols, stacks, right, out):
    me = lax.axis_index("row")
    col = lax.axis_index("col")
    held = (me % group_count) ^ col
    for row in range(rows):
        values = [ref[row, 0] for ref in stacks[:PAIR + 1]] + [ref[row] for ref in stacks[PAIR + 1:]]
        left = chosen(held, values)
        for slot in range(SLOTS):
            full = times(left, right[row, slot])
            out[row, slot, 0] = full[:, :size]
            out[row, slot, 1] = full[:, size:]

    @pl.when(held == 0)
    def _():
        for row in range(rows):
            partner = own_cols[row, 1] % rows
            for slot in range(SLOTS):
                full = times(stacks[0][partner, 1], right[partner, 1 - slot])
                out[row, slot, 0] += full[:, :size]
                out[row, slot, 1] += full[:, size:]


def finish_kernel(places, line, cols, *refs):
    count = len(places)
    own, density = refs[0], refs[1]
    commutator, section = refs[2 + count], refs[3 + count]
    slot = pl.program_id(1)
    commutator[0, 0, 0] = own[0, 0]
    for place, ref in zip(places, refs[2:2 + count]):
        @pl.when(line[place + slot] >= 0)
        def _():
            commutator[0, 0, 0] += ref[0, 0].astype(jnp.float32)
    section[0, 0, 0, 0] = density[0, 0, 0, 0] + 0.05 * commutator[0, 0, 0, 1]
    section[0, 0, 0, 1] = density[0, 0, 0, 1] - 0.05 * commutator[0, 0, 0, 0]


def body(plan, hamiltonian, density, block_cols):
    group_count = lax.axis_size("col")
    rows, _, slots, parts, size, _ = hamiltonian.shape
    smem = pl.BlockSpec(memory_space=pltpu.SMEM)
    vmem = pl.BlockSpec(memory_space=pltpu.VMEM)
    params = pltpu.CompilerParams(vmem_limit_bytes=40 * 1024 * 1024)

    device = lax.axis_index("row") * group_count + lax.axis_index("col")
    line = lax.dynamic_index_in_dim(jnp.asarray(plan.table), device, 0, keepdims=False)
    own_cols = block_cols[:, 0]
    stack = jnp.stack([hamiltonian[:, 0], density[:, 0].astype(jnp.bfloat16)], axis=2)
    stack = stack.reshape(rows, slots, 2 * parts * size, size)
    across = xor_col(stack, group_count, PAIR)
    near = xor_col(stack, group_count, 1)
    near_cols = xor_col(own_cols, group_count, 1)

    arrived = {}

    def send(turns, stacks):
        *sent, own = pl.pallas_call(
            functools.partial(terms_kernel, plan, turns, group_count, rows, size),
            out_shape=[
                jax.ShapeDtypeStruct((plan.width[turn], rows, parts, size, size), jnp.bfloat16)
                for turn in turns
            ] + [jax.ShapeDtypeStruct((rows, slots, parts, size, size), jnp.float32)],
            in_specs=[smem, smem, smem] + [vmem] * len(stacks),
            out_specs=[vmem] * (len(turns) + 1),
            scratch_shapes=[pltpu.VMEM((rows, PAIR * SLOTS, 4 * size, 2 * size), jnp.bfloat16)],
            compiler_params=params,
            name="terms_%d" % turns[0],
        )(line, own_cols, near_cols, *stacks)
        for turn, one in zip(turns, sent):
            arrived[turn] = lax.ppermute(one, ("row", "col"), plan.pairs[turn])
        return sent, own

    sent, _ = send(plan.turns[:2], [stack, near, across])
    across_first, _ = lax.optimization_barrier((across[:, 0], sent[-1]))
    diagonal = xor_col(across_first, group_count, 1)
    _, own = send(plan.turns[2:], [stack, near, across, diagonal])

    terms = []
    places = []
    for turn, one in sorted(arrived.items()):
        terms += [one, xor_col(one, group_count, 1)]
        places += [plan.find_at[turn, 0], plan.find_at[turn, 1]]

    block = (1, 1, 1, parts, size, size)

    def term_index(place, row, slot, line, cols):
        found = line[place + slot]
        return (
            jnp.maximum(found, 0),
            jnp.where(found >= 0, cols[row, slot] % rows, 0),
            0, 0, 0,
        )

    def slot_index(row, slot, line, cols):
        return (row, slot, 0, 0, 0)

    def home_index(row, slot, line, cols):
        return (row, 0, slot, 0, 0, 0)

    commutator, section = pl.pallas_call(
        functools.partial(finish_kernel, places),
        out_shape=[jax.ShapeDtypeStruct(density.shape, jnp.float32)] * 2,
        grid_spec=pltpu.PrefetchScalarGridSpec(
            num_scalar_prefetch=2,
            grid=(rows, slots),
            in_specs=[
                pl.BlockSpec((1, 1, parts, size, size), slot_index),
                pl.BlockSpec(block, home_index),
            ] + [
                pl.BlockSpec((1, 1, parts, size, size), functools.partial(term_index, place))
                for place in places
            ],
            out_specs=[pl.BlockSpec(block, home_index)] * 2,
        ),
        compiler_params=params,
        name="finish",
    )(line, own_cols, own, density, *terms)
    return commutator, section


def solution(mesh):
    plan = Plan(mesh.shape["row"], mesh.shape["col"])
    blocks = P("row", "col", None, None, None, None)
    return jax.shard_map(
        functools.partial(body, plan),
        mesh=mesh,
        in_specs=(blocks, blocks, P("row", "col", None)),
        out_specs=(blocks, blocks),
        check_vma=False,
    )
```

```python
import functools

import jax
import jax.numpy as jnp
import numpy as np
from jax import lax
from jax.experimental import pallas as pl
from jax.experimental.pallas import tpu as pltpu
from jax.sharding import PartitionSpec as P


SLOTS = 2
B1 = ()
B2 = (0,)
PAIR = 2


def xor_col(value, group_count, by):
    return lax.ppermute(value, "col", [(i, i ^ by) for i in range(group_count)])


class Plan:
    def __init__(self, row_count, group_count):
        assert group_count == 4
        self.turns = [0, 1, 2]
        self.pairs = {turn: [] for turn in self.turns}
        self.width = {turn: 0 for turn in self.turns}
        sends = {}
        finds = {}
        for row in range(row_count):
            for first in range(0, group_count, PAIR):
                for offset in range(1 - group_count, group_count):
                    if offset == 0:
                        continue
                    target = (row + offset) % row_count
                    turn, sender, side = self.way(row, first, offset, target, group_count)
                    taker = first + side
                    blocks = self.blocks(row, first, target, row_count, group_count)
                    codes = []
                    for column, slot, have in blocks:
                        place = (target, column, slot, turn, taker ^ column)
                        assert place not in finds
                        finds[place] = len(codes)
                        codes.append((column ^ sender) * SLOTS + have)
                    held = ((target % group_count) ^ sender) * SLOTS + (0 if offset > 0 else 1)
                    assert (row, sender, turn) not in sends
                    sends[row, sender, turn] = (held, codes)
                    self.pairs[turn].append(
                        (row * group_count + sender, target * group_count + taker)
                    )
                    self.width[turn] = max(self.width[turn], len(codes))
        lines = []
        for row in range(row_count):
            for col in range(group_count):
                line = []
                self.send_at = {}
                for turn in self.turns:
                    held, codes = sends.get((row, col, turn), (-1, []))
                    self.send_at[turn] = len(line)
                    line += [held] + codes + [-1] * (self.width[turn] - len(codes))
                self.find_at = {}
                for turn in self.turns:
                    for pair in range(PAIR):
                        self.find_at[turn, pair] = len(line)
                        line += [finds.get((row, col, slot, turn, pair), -1) for slot in range(SLOTS)]
                lines.append(line)
        self.table = np.asarray(lines, np.int32)

    def way(self, row, first, offset, target, group_count):
        if (target % group_count) // PAIR == (row % group_count) // PAIR:
            return 2, first + (target + (offset > 0)) % PAIR, int(offset > 0)
        return int(offset < 0), first + target % PAIR, int(abs(offset) == 2)

    def blocks(self, row, first, target, row_count, group_count):
        found = []
        for column in range(first, first + PAIR):
            mine = (column - row) % group_count
            theirs = (column - target) % group_count
            have = {(row + mine) % row_count: 0}
            if mine:
                have[(row + mine - group_count) % row_count] = 1
            for slot in range(SLOTS if theirs else 1):
                wanted = (target + theirs - group_count * slot) % row_count
                if wanted in have:
                    found.append((column, slot, have[wanted]))
        return found


def pack_kernel(energy, state, *outs):
    rows, _, slots, parts, size, _ = energy.shape
    for slot in range(slots):
        for row in range(rows):
            for part in range(parts):
                outs[slot][row, part * size:(part + 1) * size] = energy[row, 0, slot, part]
                outs[slot][row, (parts + part) * size:(parts + part + 1) * size] = state[
                    row, 0, slot, part
                ].astype(jnp.bfloat16)


def fill_right(right, row, place, stack, size):
    energy_re = stack[0 * size:1 * size]
    energy_im = stack[1 * size:2 * size]
    state_re = stack[2 * size:3 * size]
    state_im = stack[3 * size:4 * size]
    right[row, place, 0 * size:1 * size, :size] = state_re
    right[row, place, 0 * size:1 * size, size:] = state_im
    right[row, place, 1 * size:2 * size, :size] = state_im
    right[row, place, 1 * size:2 * size, size:] = -state_re
    right[row, place, 2 * size:3 * size, :size] = -energy_re
    right[row, place, 2 * size:3 * size, size:] = -energy_im
    right[row, place, 3 * size:4 * size, :size] = -energy_im
    right[row, place, 3 * size:4 * size, size:] = energy_re


def times(left, right):
    return lax.dot_general(
        left, right, (((0,), (0,)), ((), ())), preferred_element_type=jnp.float32
    )


def terms_kernel(plan, turn, held_codes, rows, size, line, own_cols, near_cols, *refs):
    columns = refs[:PAIR * SLOTS]
    targets = refs[PAIR * SLOTS:PAIR * SLOTS + len(held_codes)]
    out, right = refs[PAIR * SLOTS + len(held_codes)], refs[-1]
    for row in range(rows):
        for code in range(PAIR * SLOTS):
            fill_right(right, row, code, columns[code][row], size)
    base = plan.send_at[turn]
    held = line[base]
    for row in range(rows):
        left = targets[0][row]
        for code, ref in zip(held_codes[1:], targets[1:]):
            left = jnp.where(held == code, ref[row], left)
        for place in range(plan.width[turn]):
            code = jnp.maximum(line[base + 1 + place], 0)
            pair = code // SLOTS
            slot = code % SLOTS
            full = times(left, right[row, code]).astype(jnp.bfloat16)
            there = jnp.where(pair == 0, own_cols[row, slot], near_cols[row, slot]) % rows
            out[place, there, 0] = full[:, :size]
            out[place, there, 1] = full[:, size:]


def own_kernel(group_count, rows, size, own_cols, *refs):
    firsts = refs[SLOTS:SLOTS + group_count]
    out, right = refs[-2:]
    me = lax.axis_index("row")
    col = lax.axis_index("col")
    for row in range(rows):
        for slot in range(SLOTS):
            fill_right(right, row, slot, refs[slot][row], size)
    held = (me % group_count) ^ col
    for row in range(rows):
        left = firsts[0][row]
        for place in range(1, group_count):
            left = jnp.where(held == place, firsts[place][row], left)
        for slot in range(SLOTS):
            full = times(left, right[row, slot])
            out[row, slot, 0] = full[:, :size]
            out[row, slot, 1] = full[:, size:]

    @pl.when(held == 0)
    def _():
        for row in range(rows):
            partner = own_cols[row, 1] % rows
            for slot in range(SLOTS):
                full = times(refs[1][partner], right[partner, 1 - slot])
                out[row, slot, 0] += full[:, :size]
                out[row, slot, 1] += full[:, size:]


def finish_kernel(places, line, cols, *refs):
    count = len(places)
    own, density = refs[0], refs[1]
    commutator, section = refs[2 + count], refs[3 + count]
    slot = pl.program_id(1)
    commutator[0, 0, 0] = own[0, 0]
    for place, ref in zip(places, refs[2:2 + count]):
        @pl.when(line[place + slot] >= 0)
        def _():
            commutator[0, 0, 0] += ref[0, 0].astype(jnp.float32)
    section[0, 0, 0, 0] = density[0, 0, 0, 0] + 0.05 * commutator[0, 0, 0, 1]
    section[0, 0, 0, 1] = density[0, 0, 0, 1] - 0.05 * commutator[0, 0, 0, 0]


def body(plan, hamiltonian, density, block_cols):
    group_count = lax.axis_size("col")
    rows, _, slots, parts, size, _ = hamiltonian.shape
    smem = pl.BlockSpec(memory_space=pltpu.SMEM)
    vmem = pl.BlockSpec(memory_space=pltpu.VMEM)
    params = pltpu.CompilerParams(vmem_limit_bytes=40 * 1024 * 1024)

    device = lax.axis_index("row") * group_count + lax.axis_index("col")
    line = lax.dynamic_index_in_dim(jnp.asarray(plan.table), device, 0, keepdims=False)
    own_cols = block_cols[:, 0]
    stacks = dict(enumerate(pl.pallas_call(
        pack_kernel,
        out_shape=[jax.ShapeDtypeStruct((rows, 2 * parts * size, size), jnp.bfloat16)] * slots,
        in_specs=[vmem] * 2,
        out_specs=[vmem] * slots,
        compiler_params=params,
        name="pack",
    )(hamiltonian, density)))
    for slot in range(SLOTS):
        stacks[PAIR * SLOTS + slot] = xor_col(stacks[slot], group_count, PAIR)
        stacks[SLOTS + slot] = xor_col(stacks[slot], group_count, 1)
    near_cols = xor_col(own_cols, group_count, 1)
    columns = [stacks[code] for code in range(PAIR * SLOTS)]

    arrived = {}

    def send(turn, held_codes, after=()):
        sent = pl.pallas_call(
            functools.partial(terms_kernel, plan, turn, held_codes, rows, size),
            out_shape=jax.ShapeDtypeStruct(
                (plan.width[turn], rows, parts, size, size), jnp.bfloat16
            ),
            in_specs=[smem, smem, smem] + [vmem] * (len(columns) + len(held_codes)),
            out_specs=vmem,
            scratch_shapes=[pltpu.VMEM((rows, PAIR * SLOTS, 4 * size, 2 * size), jnp.bfloat16)],
            compiler_params=params,
            name="terms_%d" % turn,
        )(line, own_cols, near_cols, *columns, *[stacks[code] for code in held_codes])
        for other in after:
            sent, arrived[other] = lax.optimization_barrier((sent, arrived[other]))
        return sent, lax.ppermute(sent, ("row", "col"), plan.pairs[turn])

    ahead, behind = PAIR * SLOTS, PAIR * SLOTS + 1
    corner = ahead + SLOTS
    sent, arrived[0] = send(0, [0, ahead])
    first, _ = lax.optimization_barrier((stacks[ahead], sent))
    stacks[corner] = xor_col(first, group_count, 1)
    sent, arrived[1] = send(1, [1, behind], B1)
    _, arrived[2] = send(2, [1, SLOTS, behind, corner], B2)

    own = pl.pallas_call(
        functools.partial(own_kernel, group_count, rows, size),
        out_shape=jax.ShapeDtypeStruct((rows, slots, parts, size, size), jnp.float32),
        in_specs=[smem] + [vmem] * (SLOTS + group_count),
        out_specs=vmem,
        scratch_shapes=[pltpu.VMEM((rows, SLOTS, 4 * size, 2 * size), jnp.bfloat16)],
        compiler_params=params,
        name="own_terms",
    )(own_cols, stacks[0], stacks[1], stacks[0], stacks[SLOTS], stacks[ahead], stacks[corner])

    terms = []
    places = []
    swapped = None
    for turn, one in sorted(arrived.items()):
        if swapped is not None:
            one, swapped = lax.optimization_barrier((one, swapped))
            terms.append(swapped)
        swapped = xor_col(one, group_count, 1)
        terms.append(one)
        places += [plan.find_at[turn, 0], plan.find_at[turn, 1]]

    terms.append(swapped)

    block = (1, 1, 1, parts, size, size)

    def term_index(place, row, slot, line, cols):
        found = line[place + slot]
        return (
            jnp.maximum(found, 0),
            jnp.where(found >= 0, cols[row, slot] % rows, 0),
            0, 0, 0,
        )

    def slot_index(row, slot, line, cols):
        return (row, slot, 0, 0, 0)

    def home_index(row, slot, line, cols):
        return (row, 0, slot, 0, 0, 0)

    commutator, section = pl.pallas_call(
        functools.partial(finish_kernel, places),
        out_shape=[jax.ShapeDtypeStruct(density.shape, jnp.float32)] * 2,
        grid_spec=pltpu.PrefetchScalarGridSpec(
            num_scalar_prefetch=2,
            grid=(rows, slots),
            in_specs=[
                pl.BlockSpec((1, 1, parts, size, size), slot_index),
                pl.BlockSpec(block, home_index),
            ] + [
                pl.BlockSpec((1, 1, parts, size, size), functools.partial(term_index, place))
                for place in places
            ],
            out_specs=[pl.BlockSpec(block, home_index)] * 2,
        ),
        compiler_params=params,
        name="finish",
    )(line, own_cols, own, density, *terms)
    return commutator, section


def solution(mesh):
    plan = Plan(mesh.shape["row"], mesh.shape["col"])
    blocks = P("row", "col", None, None, None, None)
    return jax.shard_map(
        functools.partial(body, plan),
        mesh=mesh,
        in_specs=(blocks, blocks, P("row", "col", None)),
        out_specs=(blocks, blocks),
        check_vma=False,
    )
```

```python
import functools

import jax
import jax.numpy as jnp
import numpy as np
from jax import lax
from jax.experimental import pallas as pl
from jax.experimental.pallas import tpu as pltpu
from jax.sharding import PartitionSpec as P


SLOTS = 2
OWN = 0
CHAIN = [(0, 1)]
ORDER = (0, 1, 2)
B1 = ()
B2 = ()
PAIR = 2


def xor_col(value, group_count, by):
    return lax.ppermute(value, "col", [(i, i ^ by) for i in range(group_count)])


class Plan:
    def __init__(self, row_count, group_count):
        assert group_count == 4
        self.turns = [0, 1, 2]
        self.pairs = {turn: [] for turn in self.turns}
        self.width = {turn: 0 for turn in self.turns}
        sends = {}
        finds = {}
        for row in range(row_count):
            for first in range(0, group_count, PAIR):
                for offset in range(1 - group_count, group_count):
                    if offset == 0:
                        continue
                    target = (row + offset) % row_count
                    turn, sender, side = self.way(row, first, offset, target, group_count)
                    taker = first + side
                    blocks = self.blocks(row, first, target, row_count, group_count)
                    codes = []
                    for column, slot, have in blocks:
                        place = (target, column, slot, turn, taker ^ column)
                        assert place not in finds
                        finds[place] = len(codes)
                        codes.append((column ^ sender) * SLOTS + have)
                    held = ((target % group_count) ^ sender) * SLOTS + (0 if offset > 0 else 1)
                    assert (row, sender, turn) not in sends
                    sends[row, sender, turn] = (held, codes)
                    self.pairs[turn].append(
                        (row * group_count + sender, target * group_count + taker)
                    )
                    self.width[turn] = max(self.width[turn], len(codes))
        lines = []
        for row in range(row_count):
            for col in range(group_count):
                line = []
                self.send_at = {}
                for turn in self.turns:
                    held, codes = sends.get((row, col, turn), (-1, []))
                    self.send_at[turn] = len(line)
                    line += [held] + codes + [-1] * (self.width[turn] - len(codes))
                self.find_at = {}
                for turn in self.turns:
                    for pair in range(PAIR):
                        self.find_at[turn, pair] = len(line)
                        line += [finds.get((row, col, slot, turn, pair), -1) for slot in range(SLOTS)]
                lines.append(line)
        self.table = np.asarray(lines, np.int32)

    def way(self, row, first, offset, target, group_count):
        if (target % group_count) // PAIR == (row % group_count) // PAIR:
            return 2, first + (target + (offset > 0)) % PAIR, int(offset > 0)
        return int(offset < 0), first + target % PAIR, int(abs(offset) == 2)

    def blocks(self, row, first, target, row_count, group_count):
        found = []
        for column in range(first, first + PAIR):
            mine = (column - row) % group_count
            theirs = (column - target) % group_count
            have = {(row + mine) % row_count: 0}
            if mine:
                have[(row + mine - group_count) % row_count] = 1
            for slot in range(SLOTS if theirs else 1):
                wanted = (target + theirs - group_count * slot) % row_count
                if wanted in have:
                    found.append((column, slot, have[wanted]))
        return found


def same_pair(group_count):
    pair = (lax.axis_index("row") % group_count) // PAIR
    return (pair == lax.axis_index("col") // PAIR).astype(jnp.int32)


def pack_kernel(group_count, energy, state, *outs):
    rows, _, slots, parts, size, _ = energy.shape
    crossing = same_pair(group_count)
    for row in range(rows):
        for part in range(parts):
            here = pl.ds(part * size, size)
            there = pl.ds((parts + part) * size, size)
            outs[slots][row, here] = energy[row, 0, crossing, part]
            outs[slots][row, there] = state[row, 0, crossing, part].astype(jnp.bfloat16)
    for slot in range(slots):
        for row in range(rows):
            for part in range(parts):
                outs[slot][row, part * size:(part + 1) * size] = energy[row, 0, slot, part]
                outs[slot][row, (parts + part) * size:(parts + part + 1) * size] = state[
                    row, 0, slot, part
                ].astype(jnp.bfloat16)


def fill_right(right, row, place, stack, size):
    energy_re = stack[0 * size:1 * size]
    energy_im = stack[1 * size:2 * size]
    state_re = stack[2 * size:3 * size]
    state_im = stack[3 * size:4 * size]
    right[row, place, 0 * size:1 * size, :size] = state_re
    right[row, place, 0 * size:1 * size, size:] = state_im
    right[row, place, 1 * size:2 * size, :size] = state_im
    right[row, place, 1 * size:2 * size, size:] = -state_re
    right[row, place, 2 * size:3 * size, :size] = -energy_re
    right[row, place, 2 * size:3 * size, size:] = -energy_im
    right[row, place, 3 * size:4 * size, :size] = -energy_im
    right[row, place, 3 * size:4 * size, size:] = energy_re


def times(left, right):
    return lax.dot_general(
        left, right, (((0,), (0,)), ((), ())), preferred_element_type=jnp.float32
    )


def terms_kernel(plan, turn, held_codes, rows, size, line, own_cols, near_cols, *refs):
    columns = refs[:PAIR * SLOTS]
    targets = refs[PAIR * SLOTS:PAIR * SLOTS + len(held_codes)]
    out, right = refs[PAIR * SLOTS + len(held_codes)], refs[-1]
    for row in range(rows):
        for code in range(PAIR * SLOTS):
            fill_right(right, row, code, columns[code][row], size)
    base = plan.send_at[turn]
    held = line[base]
    for row in range(rows):
        left = targets[0][row]
        for code, ref in zip(held_codes[1:], targets[1:]):
            left = jnp.where(held == code, ref[row], left)
        for place in range(plan.width[turn]):
            code = jnp.maximum(line[base + 1 + place], 0)
            pair = code // SLOTS
            slot = code % SLOTS
            full = times(left, right[row, code]).astype(jnp.bfloat16)
            there = jnp.where(pair == 0, own_cols[row, slot], near_cols[row, slot]) % rows
            out[place, there, 0] = full[:, :size]
            out[place, there, 1] = full[:, size:]


def own_kernel(group_count, rows, size, own_cols, *refs):
    firsts = refs[SLOTS:SLOTS + group_count]
    out, right = refs[-2:]
    me = lax.axis_index("row")
    col = lax.axis_index("col")
    for row in range(rows):
        for slot in range(SLOTS):
            fill_right(right, row, slot, refs[slot][row], size)
    held = (me % group_count) ^ col
    for row in range(rows):
        left = firsts[0][row]
        for place in range(1, group_count):
            left = jnp.where(held == place, firsts[place][row], left)
        for slot in range(SLOTS):
            full = times(left, right[row, slot])
            out[row, slot, 0] = full[:, :size]
            out[row, slot, 1] = full[:, size:]

    @pl.when(held == 0)
    def _():
        for row in range(rows):
            partner = own_cols[row, 1] % rows
            for slot in range(SLOTS):
                full = times(refs[1][partner], right[partner, 1 - slot])
                out[row, slot, 0] += full[:, :size]
                out[row, slot, 1] += full[:, size:]


def finish_kernel(places, line, cols, own, density, *refs):
    terms = refs[:len(places)]
    commutator, section = refs[len(places):]
    rows, slots = own.shape[:2]
    for row in range(rows):
        for slot in range(slots):
            total = own[row, slot]
            for place, ref in zip(places, terms):
                found = line[place + slot]
                block = ref[jnp.maximum(found, 0), cols[row, slot] % rows]
                total += jnp.where(found >= 0, block, 0.0).astype(jnp.float32)
            commutator[row, 0, slot] = total
            section[row, 0, slot, 0] = density[row, 0, slot, 0] + 0.05 * total[1]
            section[row, 0, slot, 1] = density[row, 0, slot, 1] - 0.05 * total[0]


def body(plan, hamiltonian, density, block_cols):
    group_count = lax.axis_size("col")
    rows, _, slots, parts, size, _ = hamiltonian.shape
    smem = pl.BlockSpec(memory_space=pltpu.SMEM)
    vmem = pl.BlockSpec(memory_space=pltpu.VMEM)
    params = pltpu.CompilerParams(vmem_limit_bytes=40 * 1024 * 1024)

    device = lax.axis_index("row") * group_count + lax.axis_index("col")
    line = lax.dynamic_index_in_dim(jnp.asarray(plan.table), device, 0, keepdims=False)
    own_cols = block_cols[:, 0]
    own_0, own_1, first_out = pl.pallas_call(
        functools.partial(pack_kernel, group_count),
        out_shape=[jax.ShapeDtypeStruct((rows, 2 * parts * size, size), jnp.bfloat16)] * 3,
        in_specs=[vmem] * 2,
        out_specs=[vmem] * 3,
        compiler_params=params,
        name="pack",
    )(hamiltonian, density)
    first_in = xor_col(first_out, group_count, PAIR)
    near_0 = xor_col(own_0, group_count, 1)
    near_1 = xor_col(own_1, group_count, 1)
    second_out = jnp.where(same_pair(group_count) == 1, near_0, own_1)
    second_in = xor_col(second_out, group_count, PAIR)
    columns = [own_0, own_1, near_0, near_1]
    near_cols = xor_col(own_cols, group_count, 1)

    arrived = {}

    def send(turn, held, after=()):
        sent = pl.pallas_call(
            functools.partial(terms_kernel, plan, turn, list(held), rows, size),
            out_shape=jax.ShapeDtypeStruct(
                (plan.width[turn], rows, parts, size, size), jnp.bfloat16
            ),
            in_specs=[smem, smem, smem] + [vmem] * (len(columns) + len(held)),
            out_specs=vmem,
            scratch_shapes=[pltpu.VMEM((rows, PAIR * SLOTS, 4 * size, 2 * size), jnp.bfloat16)],
            compiler_params=params,
            name="terms_%d" % turn,
        )(line, own_cols, near_cols, *columns, *held.values())
        for other in after:
            sent, arrived[other] = lax.optimization_barrier((sent, arrived[other]))
        return sent, lax.ppermute(sent, ("row", "col"), plan.pairs[turn])

    _, arrived[0] = send(0, {0: own_0, 4: first_in})
    _, arrived[1] = send(1, {1: own_1, 5: second_in}, B1)
    sent, arrived[2] = send(2, {1: own_1, 2: near_0, 5: first_in, 6: second_in}, B2)
    late, _ = lax.optimization_barrier((second_in, sent))
    late = xor_col(late, group_count, 1)

    own = pl.pallas_call(
        functools.partial(own_kernel, group_count, rows, size),
        out_shape=jax.ShapeDtypeStruct((rows, slots, parts, size, size), jnp.float32),
        in_specs=[smem] + [vmem] * (SLOTS + group_count),
        out_specs=vmem,
        scratch_shapes=[pltpu.VMEM((rows, SLOTS, 4 * size, 2 * size), jnp.bfloat16)],
        compiler_params=params,
        name="own_terms",
    )(own_cols, own_0, own_1, own_0, near_0, late, second_in)

    terms = []
    places = []
    swapped = {}
    for turn in ORDER:
        one = arrived[turn]
        for before, after in CHAIN:
            if after == turn:
                one, swapped[before] = lax.optimization_barrier((one, swapped[before]))
        if turn == OWN:
            one, own = lax.optimization_barrier((one, own))
        arrived[turn] = one
        swapped[turn] = xor_col(one, group_count, 1)
    for turn in plan.turns:
        terms += [arrived[turn], swapped[turn]]
        places += [plan.find_at[turn, 0], plan.find_at[turn, 1]]

    commutator, section = pl.pallas_call(
        functools.partial(finish_kernel, places),
        out_shape=[jax.ShapeDtypeStruct(density.shape, jnp.float32)] * 2,
        in_specs=[smem] * 2 + [vmem] * (2 + len(terms)),
        out_specs=[vmem] * 2,
        compiler_params=params,
        name="finish",
    )(line, own_cols, own, density, *terms)
    return commutator, section


def solution(mesh):
    plan = Plan(mesh.shape["row"], mesh.shape["col"])
    blocks = P("row", "col", None, None, None, None)
    return jax.shard_map(
        functools.partial(body, plan),
        mesh=mesh,
        in_specs=(blocks, blocks, P("row", "col", None)),
        out_specs=(blocks, blocks),
        check_vma=False,
    )
```

```python
import functools

import jax
import jax.numpy as jnp
import numpy as np
from jax import lax
from jax.experimental import pallas as pl
from jax.experimental.pallas import tpu as pltpu
from jax.sharding import PartitionSpec as P


SLOTS = 2
PAIR = 2


def xor_col(value, group_count, by):
    return lax.ppermute(value, "col", [(i, i ^ by) for i in range(group_count)])


class Plan:
    def __init__(self, row_count, group_count):
        assert group_count == 4
        self.turns = [0, 1, 2, 3]
        self.direct = [3]
        self.pairs = {turn: [] for turn in self.turns}
        self.width = {turn: 0 for turn in self.turns}
        sends = {}
        finds = {}
        for row in range(row_count):
            for first in range(0, group_count, PAIR):
                for offset in range(1 - group_count, group_count):
                    if offset == 0:
                        continue
                    target = (row + offset) % row_count
                    blocks = self.blocks(row, first, target, row_count, group_count)
                    for turn, sender, taker, columns in self.ways(row, first, offset, target, group_count):
                        codes = []
                        for column, slot, have in blocks:
                            if column in columns:
                                finds[target, column, slot, turn, taker ^ column] = len(codes)
                                codes.append((column ^ sender) * SLOTS + have)
                        held = ((target % group_count) ^ sender) * SLOTS + (0 if offset > 0 else 1)
                        assert (row, sender, turn) not in sends
                        sends[row, sender, turn] = (held, codes)
                        self.pairs[turn].append(
                            (row * group_count + sender, target * group_count + taker)
                        )
                        self.width[turn] = max(self.width[turn], len(codes))
        lines = []
        for row in range(row_count):
            for col in range(group_count):
                line = []
                self.send_at = {}
                for turn in self.turns:
                    held, codes = sends.get((row, col, turn), (-1, []))
                    self.send_at[turn] = len(line)
                    line += [held] + codes + [-1] * (self.width[turn] - len(codes))
                self.find_at = {}
                for turn in self.turns:
                    for pair in range(PAIR):
                        self.find_at[turn, pair] = len(line)
                        line += [finds.get((row, col, slot, turn, pair), -1) for slot in range(SLOTS)]
                lines.append(line)
        self.table = np.asarray(lines, np.int32)

    def ways(self, row, first, offset, target, group_count):
        both = (first, first + 1)
        if (target % group_count) // PAIR != (row % group_count) // PAIR:
            side = int(abs(offset) == 2)
            return [(int(offset < 0), first + target % PAIR, first + side, both)]
        behind = int(offset < 0)
        sender = first + (target + 1 - behind) % PAIR
        if (target % group_count) // PAIR == first // PAIR:
            return [(2, sender, first + behind, both)]
        return [(2 + (side ^ behind), sender, first + side, (first + side,)) for side in range(PAIR)]

    def blocks(self, row, first, target, row_count, group_count):
        found = []
        for column in range(first, first + PAIR):
            mine = (column - row) % group_count
            theirs = (column - target) % group_count
            have = {(row + mine) % row_count: 0}
            if mine:
                have[(row + mine - group_count) % row_count] = 1
            for slot in range(SLOTS if theirs else 1):
                wanted = (target + theirs - group_count * slot) % row_count
                if wanted in have:
                    found.append((column, slot, have[wanted]))
        return found


def same_pair(group_count):
    pair = (lax.axis_index("row") % group_count) // PAIR
    return (pair == lax.axis_index("col") // PAIR).astype(jnp.int32)


def pack_kernel(group_count, energy, state, *outs):
    rows, _, slots, parts, size, _ = energy.shape
    crossing = same_pair(group_count)
    for row in range(rows):
        for part in range(parts):
            here = pl.ds(part * size, size)
            there = pl.ds((parts + part) * size, size)
            outs[slots][row, here] = energy[row, 0, crossing, part]
            outs[slots][row, there] = state[row, 0, crossing, part].astype(jnp.bfloat16)
    for slot in range(slots):
        for row in range(rows):
            for part in range(parts):
                outs[slot][row, part * size:(part + 1) * size] = energy[row, 0, slot, part]
                outs[slot][row, (parts + part) * size:(parts + part + 1) * size] = state[
                    row, 0, slot, part
                ].astype(jnp.bfloat16)


def fill_right(right, row, place, stack, size):
    energy_re = stack[0 * size:1 * size]
    energy_im = stack[1 * size:2 * size]
    state_re = stack[2 * size:3 * size]
    state_im = stack[3 * size:4 * size]
    right[row, place, 0 * size:1 * size, :size] = state_re
    right[row, place, 0 * size:1 * size, size:] = state_im
    right[row, place, 1 * size:2 * size, :size] = state_im
    right[row, place, 1 * size:2 * size, size:] = -state_re
    right[row, place, 2 * size:3 * size, :size] = -energy_re
    right[row, place, 2 * size:3 * size, size:] = -energy_im
    right[row, place, 3 * size:4 * size, :size] = -energy_im
    right[row, place, 3 * size:4 * size, size:] = energy_re


def times(left, right):
    return lax.dot_general(
        left, right, (((0,), (0,)), ((), ())), preferred_element_type=jnp.float32
    )


def terms_kernel(plan, turns, held_codes, rows, size, line, own_cols, near_cols, *refs):
    columns = refs[:PAIR * SLOTS]
    targets = refs[PAIR * SLOTS:PAIR * SLOTS + len(held_codes)]
    outs, right = refs[-len(turns) - 1:-1], refs[-1]
    for row in range(rows):
        for code in range(PAIR * SLOTS):
            fill_right(right, row, code, columns[code][row], size)
    for row in range(rows):
        held = line[plan.send_at[turns[0]]]
        left = targets[0][row]
        for code, ref in zip(held_codes[1:], targets[1:]):
            left = jnp.where(held == code, ref[row], left)
        for turn, out in zip(turns, outs):
            for place in range(plan.width[turn]):
                code = jnp.maximum(line[plan.send_at[turn] + 1 + place], 0)
                pair = code // SLOTS
                slot = code % SLOTS
                full = times(left, right[row, code]).astype(jnp.bfloat16)
                there = jnp.where(pair == 0, own_cols[row, slot], near_cols[row, slot]) % rows
                out[place, there, 0] = full[:, :size]
                out[place, there, 1] = full[:, size:]


def own_kernel(group_count, rows, size, own_cols, *refs):
    firsts = refs[SLOTS:SLOTS + group_count]
    out, right = refs[-2:]
    me = lax.axis_index("row")
    col = lax.axis_index("col")
    for row in range(rows):
        for slot in range(SLOTS):
            fill_right(right, row, slot, refs[slot][row], size)
    held = (me % group_count) ^ col
    for row in range(rows):
        left = firsts[0][row]
        for place in range(1, group_count):
            left = jnp.where(held == place, firsts[place][row], left)
        for slot in range(SLOTS):
            full = times(left, right[row, slot])
            out[row, slot, 0] = full[:, :size]
            out[row, slot, 1] = full[:, size:]

    @pl.when(held == 0)
    def _():
        for row in range(rows):
            partner = own_cols[row, 1] % rows
            for slot in range(SLOTS):
                full = times(refs[1][partner], right[partner, 1 - slot])
                out[row, slot, 0] += full[:, :size]
                out[row, slot, 1] += full[:, size:]


def finish_kernel(places, line, cols, own, density, *refs):
    terms = refs[:len(places)]
    commutator, section = refs[len(places):]
    rows, slots = own.shape[:2]
    for row in range(rows):
        for slot in range(slots):
            total = own[row, slot]
            for place, ref in zip(places, terms):
                found = line[place + slot]
                block = ref[jnp.maximum(found, 0), cols[row, slot] % rows]
                total += jnp.where(found >= 0, block, 0.0).astype(jnp.float32)
            commutator[row, 0, slot] = total
            section[row, 0, slot, 0] = density[row, 0, slot, 0] + 0.05 * total[1]
            section[row, 0, slot, 1] = density[row, 0, slot, 1] - 0.05 * total[0]


def body(plan, hamiltonian, density, block_cols):
    group_count = lax.axis_size("col")
    rows, _, slots, parts, size, _ = hamiltonian.shape
    smem = pl.BlockSpec(memory_space=pltpu.SMEM)
    vmem = pl.BlockSpec(memory_space=pltpu.VMEM)
    params = pltpu.CompilerParams(vmem_limit_bytes=40 * 1024 * 1024)

    device = lax.axis_index("row") * group_count + lax.axis_index("col")
    line = lax.dynamic_index_in_dim(jnp.asarray(plan.table), device, 0, keepdims=False)
    own_cols = block_cols[:, 0]
    own_0, own_1, first_out = pl.pallas_call(
        functools.partial(pack_kernel, group_count),
        out_shape=[jax.ShapeDtypeStruct((rows, 2 * parts * size, size), jnp.bfloat16)] * 3,
        in_specs=[vmem] * 2,
        out_specs=[vmem] * 3,
        compiler_params=params,
        name="pack",
    )(hamiltonian, density)
    first_in = xor_col(first_out, group_count, PAIR)
    near_0 = xor_col(own_0, group_count, 1)
    near_1 = xor_col(own_1, group_count, 1)
    second_out = jnp.where(same_pair(group_count) == 1, near_0, own_1)
    second_in = xor_col(second_out, group_count, PAIR)
    columns = [own_0, own_1, near_0, near_1]
    near_cols = xor_col(own_cols, group_count, 1)

    arrived = {}

    def send(turns, held):
        sent = pl.pallas_call(
            functools.partial(terms_kernel, plan, turns, list(held), rows, size),
            out_shape=[
                jax.ShapeDtypeStruct((plan.width[turn], rows, parts, size, size), jnp.bfloat16)
                for turn in turns
            ],
            in_specs=[smem, smem, smem] + [vmem] * (len(columns) + len(held)),
            out_specs=[vmem] * len(turns),
            scratch_shapes=[pltpu.VMEM((rows, PAIR * SLOTS, 4 * size, 2 * size), jnp.bfloat16)],
            compiler_params=params,
            name="terms_%d" % turns[0],
        )(line, own_cols, near_cols, *columns, *held.values())
        for turn, one in zip(turns, sent):
            arrived[turn] = lax.ppermute(one, ("row", "col"), plan.pairs[turn])
        return sent

    send([0], {0: own_0, 4: first_in})
    send([1], {1: own_1, 5: second_in})
    sent = send([2, 3], {1: own_1, 2: near_0, 5: first_in, 6: second_in})[0]
    late, _ = lax.optimization_barrier((second_in, sent))
    late = xor_col(late, group_count, 1)

    own = pl.pallas_call(
        functools.partial(own_kernel, group_count, rows, size),
        out_shape=jax.ShapeDtypeStruct((rows, slots, parts, size, size), jnp.float32),
        in_specs=[smem] + [vmem] * (SLOTS + group_count),
        out_specs=vmem,
        scratch_shapes=[pltpu.VMEM((rows, SLOTS, 4 * size, 2 * size), jnp.bfloat16)],
        compiler_params=params,
        name="own_terms",
    )(own_cols, own_0, own_1, own_0, near_0, late, second_in)

    arrived[0], own = lax.optimization_barrier((arrived[0], own))
    arrived[2], arrived[3] = lax.optimization_barrier((arrived[2], arrived[3]))
    swapped = {
        turn: xor_col(arrived[turn], group_count, 1)
        for turn in plan.turns if turn not in plan.direct
    }
    terms = [arrived[turn] for turn in plan.turns] + [swapped[turn] for turn in swapped]
    places = [plan.find_at[turn, 0] for turn in plan.turns]
    places += [plan.find_at[turn, 1] for turn in swapped]

    commutator, section = pl.pallas_call(
        functools.partial(finish_kernel, places),
        out_shape=[jax.ShapeDtypeStruct(density.shape, jnp.float32)] * 2,
        in_specs=[smem] * 2 + [vmem] * (2 + len(terms)),
        out_specs=[vmem] * 2,
        compiler_params=params,
        name="finish",
    )(line, own_cols, own, density, *terms)
    return commutator, section


def solution(mesh):
    plan = Plan(mesh.shape["row"], mesh.shape["col"])
    blocks = P("row", "col", None, None, None, None)
    return jax.shard_map(
        functools.partial(body, plan),
        mesh=mesh,
        in_specs=(blocks, blocks, P("row", "col", None)),
        out_specs=(blocks, blocks),
        check_vma=False,
    )
```

```python
import functools

import jax
import jax.numpy as jnp
import numpy as np
from jax import lax
from jax.experimental import pallas as pl
from jax.experimental.pallas import tpu as pltpu
from jax.sharding import PartitionSpec as P


SLOTS = 2
PAIR = 2


def xor_col(value, group_count, by):
    return lax.ppermute(value, "col", [(i, i ^ by) for i in range(group_count)])


class Plan:
    def __init__(self, row_count, group_count):
        assert group_count == 4
        self.turns = [0, 1, 2, 3]
        self.direct = [3]
        self.pairs = {turn: [] for turn in self.turns}
        self.width = {turn: 0 for turn in self.turns}
        sends = {}
        finds = {}
        for row in range(row_count):
            for first in range(0, group_count, PAIR):
                for offset in range(1 - group_count, group_count):
                    if offset == 0:
                        continue
                    target = (row + offset) % row_count
                    blocks = self.blocks(row, first, target, row_count, group_count)
                    for turn, sender, taker, columns in self.ways(row, first, offset, target, group_count):
                        codes = []
                        for column, slot, have in blocks:
                            if column in columns:
                                finds[target, column, slot, turn, taker ^ column] = len(codes)
                                codes.append((column ^ sender) * SLOTS + have)
                        held = ((target % group_count) ^ sender) * SLOTS + (0 if offset > 0 else 1)
                        assert (row, sender, turn) not in sends
                        sends[row, sender, turn] = (held, codes)
                        self.pairs[turn].append(
                            (row * group_count + sender, target * group_count + taker)
                        )
                        self.width[turn] = max(self.width[turn], len(codes))
        lines = []
        for row in range(row_count):
            for col in range(group_count):
                line = []
                self.send_at = {}
                for turn in self.turns:
                    held, codes = sends.get((row, col, turn), (-1, []))
                    self.send_at[turn] = len(line)
                    line += [held] + codes + [-1] * (self.width[turn] - len(codes))
                self.find_at = {}
                for turn in self.turns:
                    for pair in range(PAIR):
                        self.find_at[turn, pair] = len(line)
                        line += [finds.get((row, col, slot, turn, pair), -1) for slot in range(SLOTS)]
                lines.append(line)
        self.table = np.asarray(lines, np.int32)

    def ways(self, row, first, offset, target, group_count):
        both = (first, first + 1)
        if (target % group_count) // PAIR != (row % group_count) // PAIR:
            side = int(abs(offset) == 2)
            return [(int(offset < 0), first + target % PAIR, first + side, both)]
        behind = int(offset < 0)
        sender = first + (target + 1 - behind) % PAIR
        if (target % group_count) // PAIR == first // PAIR:
            return [(2, sender, first + behind, both)]
        return [(2 + (side ^ behind), sender, first + side, (first + side,)) for side in range(PAIR)]

    def blocks(self, row, first, target, row_count, group_count):
        found = []
        for column in range(first, first + PAIR):
            mine = (column - row) % group_count
            theirs = (column - target) % group_count
            have = {(row + mine) % row_count: 0}
            if mine:
                have[(row + mine - group_count) % row_count] = 1
            for slot in range(SLOTS if theirs else 1):
                wanted = (target + theirs - group_count * slot) % row_count
                if wanted in have:
                    found.append((column, slot, have[wanted]))
        return found


def same_pair(group_count):
    pair = (lax.axis_index("row") % group_count) // PAIR
    return (pair == lax.axis_index("col") // PAIR).astype(jnp.int32)


def pack_kernel(group_count, energy, state, *outs):
    rows, _, slots, parts, size, _ = energy.shape
    crossing = same_pair(group_count)
    for row in range(rows):
        for part in range(parts):
            here = pl.ds(part * size, size)
            there = pl.ds((parts + part) * size, size)
            outs[slots][row, here] = energy[row, 0, crossing, part]
            outs[slots][row, there] = state[row, 0, crossing, part].astype(jnp.bfloat16)
    for slot in range(slots):
        for row in range(rows):
            for part in range(parts):
                outs[slot][row, part * size:(part + 1) * size] = energy[row, 0, slot, part]
                outs[slot][row, (parts + part) * size:(parts + part + 1) * size] = state[
                    row, 0, slot, part
                ].astype(jnp.bfloat16)


def fill_right(right, row, place, stack, size):
    energy_re = stack[0 * size:1 * size]
    energy_im = stack[1 * size:2 * size]
    state_re = stack[2 * size:3 * size]
    state_im = stack[3 * size:4 * size]
    right[row, place, 0 * size:1 * size, :size] = state_re
    right[row, place, 0 * size:1 * size, size:] = state_im
    right[row, place, 1 * size:2 * size, :size] = state_im
    right[row, place, 1 * size:2 * size, size:] = -state_re
    right[row, place, 2 * size:3 * size, :size] = -energy_re
    right[row, place, 2 * size:3 * size, size:] = -energy_im
    right[row, place, 3 * size:4 * size, :size] = -energy_im
    right[row, place, 3 * size:4 * size, size:] = energy_re


def times(left, right):
    return lax.dot_general(
        left, right, (((0,), (0,)), ((), ())), preferred_element_type=jnp.float32
    )


def terms_kernel(plan, turns, held_codes, rows, size, line, own_cols, near_cols, *refs):
    columns = refs[:PAIR * SLOTS]
    targets = refs[PAIR * SLOTS:PAIR * SLOTS + len(held_codes)]
    outs, right = refs[-len(turns) - 1:-1], refs[-1]
    for row in range(rows):
        for code in range(PAIR * SLOTS):
            fill_right(right, row, code, columns[code][row], size)
    for row in range(rows):
        held = line[plan.send_at[turns[0]]]
        left = targets[0][row]
        for code, ref in zip(held_codes[1:], targets[1:]):
            left = jnp.where(held == code, ref[row], left)
        for turn, out in zip(turns, outs):
            for place in range(plan.width[turn]):
                code = jnp.maximum(line[plan.send_at[turn] + 1 + place], 0)
                pair = code // SLOTS
                slot = code % SLOTS
                full = times(left, right[row, code]).astype(jnp.bfloat16)
                there = jnp.where(pair == 0, own_cols[row, slot], near_cols[row, slot]) % rows
                out[place, there, 0] = full[:, :size]
                out[place, there, 1] = full[:, size:]


def own_kernel(group_count, rows, size, places, line, own_cols, *refs):
    firsts = refs[SLOTS:SLOTS + group_count]
    early = refs[SLOTS + group_count:-2]
    out, right = refs[-2:]
    me = lax.axis_index("row")
    col = lax.axis_index("col")
    for row in range(rows):
        for slot in range(SLOTS):
            fill_right(right, row, slot, refs[slot][row], size)
    held = (me % group_count) ^ col
    for row in range(rows):
        left = firsts[0][row]
        for place in range(1, group_count):
            left = jnp.where(held == place, firsts[place][row], left)
        for slot in range(SLOTS):
            full = times(left, right[row, slot])
            out[row, slot, 0] = full[:, :size]
            out[row, slot, 1] = full[:, size:]

    @pl.when(held == 0)
    def _():
        for row in range(rows):
            partner = own_cols[row, 1] % rows
            for slot in range(SLOTS):
                full = times(refs[1][partner], right[partner, 1 - slot])
                out[row, slot, 0] += full[:, :size]
                out[row, slot, 1] += full[:, size:]

    for row in range(rows):
        for slot in range(SLOTS):
            out[row, slot] = add_terms(out[row, slot], row, slot, places, line, own_cols, early)


def add_terms(total, row, slot, places, line, cols, terms):
    for place, ref in zip(places, terms):
        found = line[place + slot]
        block = ref[jnp.maximum(found, 0), cols[row, slot] % cols.shape[0]]
        total += jnp.where(found >= 0, block, 0.0).astype(jnp.float32)
    return total


def finish_kernel(places, line, cols, own, density, *refs):
    terms = refs[:len(places)]
    commutator, section = refs[len(places):]
    rows, slots = own.shape[:2]
    for row in range(rows):
        for slot in range(slots):
            total = add_terms(own[row, slot], row, slot, places, line, cols, terms)
            commutator[row, 0, slot] = total
            section[row, 0, slot, 0] = density[row, 0, slot, 0] + 0.05 * total[1]
            section[row, 0, slot, 1] = density[row, 0, slot, 1] - 0.05 * total[0]


def body(plan, hamiltonian, density, block_cols):
    group_count = lax.axis_size("col")
    rows, _, slots, parts, size, _ = hamiltonian.shape
    smem = pl.BlockSpec(memory_space=pltpu.SMEM)
    vmem = pl.BlockSpec(memory_space=pltpu.VMEM)
    params = pltpu.CompilerParams(vmem_limit_bytes=40 * 1024 * 1024)

    device = lax.axis_index("row") * group_count + lax.axis_index("col")
    line = lax.dynamic_index_in_dim(jnp.asarray(plan.table), device, 0, keepdims=False)
    own_cols = block_cols[:, 0]
    own_0, own_1, first_out = pl.pallas_call(
        functools.partial(pack_kernel, group_count),
        out_shape=[jax.ShapeDtypeStruct((rows, 2 * parts * size, size), jnp.bfloat16)] * 3,
        in_specs=[vmem] * 2,
        out_specs=[vmem] * 3,
        compiler_params=params,
        name="pack",
    )(hamiltonian, density)
    first_in = xor_col(first_out, group_count, PAIR)
    near_0 = xor_col(own_0, group_count, 1)
    near_1 = xor_col(own_1, group_count, 1)
    second_out = jnp.where(same_pair(group_count) == 1, near_0, own_1)
    second_in = xor_col(second_out, group_count, PAIR)
    columns = [own_0, own_1, near_0, near_1]
    near_cols = xor_col(own_cols, group_count, 1)

    arrived = {}

    def send(turns, held):
        sent = pl.pallas_call(
            functools.partial(terms_kernel, plan, turns, list(held), rows, size),
            out_shape=[
                jax.ShapeDtypeStruct((plan.width[turn], rows, parts, size, size), jnp.bfloat16)
                for turn in turns
            ],
            in_specs=[smem, smem, smem] + [vmem] * (len(columns) + len(held)),
            out_specs=[vmem] * len(turns),
            scratch_shapes=[pltpu.VMEM((rows, PAIR * SLOTS, 4 * size, 2 * size), jnp.bfloat16)],
            compiler_params=params,
            name="terms_%d" % turns[0],
        )(line, own_cols, near_cols, *columns, *held.values())
        for turn, one in zip(turns, sent):
            arrived[turn] = lax.ppermute(one, ("row", "col"), plan.pairs[turn])
        return sent

    send([0], {0: own_0, 4: first_in})
    send([1], {1: own_1, 5: second_in})
    sent = send([2, 3], {1: own_1, 2: near_0, 5: first_in, 6: second_in})[0]
    late, _ = lax.optimization_barrier((second_in, sent))
    late = xor_col(late, group_count, 1)

    swapped = {0: xor_col(arrived[0], group_count, 1)}
    early = [arrived[0], swapped[0]]
    places = [plan.find_at[0, 0], plan.find_at[0, 1]]
    own = pl.pallas_call(
        functools.partial(own_kernel, group_count, rows, size, places),
        out_shape=jax.ShapeDtypeStruct((rows, slots, parts, size, size), jnp.float32),
        in_specs=[smem, smem] + [vmem] * (SLOTS + group_count + len(early)),
        out_specs=vmem,
        scratch_shapes=[pltpu.VMEM((rows, SLOTS, 4 * size, 2 * size), jnp.bfloat16)],
        compiler_params=params,
        name="own_terms",
    )(line, own_cols, own_0, own_1, own_0, near_0, late, second_in, *early)

    arrived[1], arrived[3] = lax.optimization_barrier((arrived[1], arrived[3]))
    swapped[1] = xor_col(arrived[1], group_count, 1)
    swapped[2] = xor_col(arrived[2], group_count, 1)
    terms = [arrived[1], arrived[2], arrived[3], swapped[1], swapped[2]]
    places = [plan.find_at[turn, 0] for turn in (1, 2, 3)] + [plan.find_at[turn, 1] for turn in (1, 2)]

    commutator, section = pl.pallas_call(
        functools.partial(finish_kernel, places),
        out_shape=[jax.ShapeDtypeStruct(density.shape, jnp.float32)] * 2,
        in_specs=[smem] * 2 + [vmem] * (2 + len(terms)),
        out_specs=[vmem] * 2,
        compiler_params=params,
        name="finish",
    )(line, own_cols, own, density, *terms)
    return commutator, section


def solution(mesh):
    plan = Plan(mesh.shape["row"], mesh.shape["col"])
    blocks = P("row", "col", None, None, None, None)
    return jax.shard_map(
        functools.partial(body, plan),
        mesh=mesh,
        in_specs=(blocks, blocks, P("row", "col", None)),
        out_specs=(blocks, blocks),
        check_vma=False,
    )
```

```python
import functools

import jax
import jax.numpy as jnp
import numpy as np
from jax import lax
from jax.experimental import pallas as pl
from jax.experimental.pallas import tpu as pltpu
from jax.sharding import PartitionSpec as P


SLOTS = 2
PAIR = 2


def xor_col(value, group_count, by):
    return lax.ppermute(value, "col", [(i, i ^ by) for i in range(group_count)])


class Plan:
    def __init__(self, row_count, group_count):
        assert group_count == 4
        self.turns = [0, 1, 2, 3]
        self.direct = [3]
        self.pairs = {turn: [] for turn in self.turns}
        self.width = {turn: 0 for turn in self.turns}
        sends = {}
        finds = {}
        for row in range(row_count):
            for first in range(0, group_count, PAIR):
                for offset in range(1 - group_count, group_count):
                    if offset == 0:
                        continue
                    target = (row + offset) % row_count
                    blocks = self.blocks(row, first, target, row_count, group_count)
                    for turn, sender, taker, columns in self.ways(row, first, offset, target, group_count):
                        codes = []
                        for column, slot, have in blocks:
                            if column in columns:
                                finds[target, column, slot, turn, taker ^ column] = len(codes)
                                codes.append((column ^ sender) * SLOTS + have)
                        held = ((target % group_count) ^ sender) * SLOTS + (0 if offset > 0 else 1)
                        assert (row, sender, turn) not in sends
                        sends[row, sender, turn] = (held, codes)
                        self.pairs[turn].append(
                            (row * group_count + sender, target * group_count + taker)
                        )
                        self.width[turn] = max(self.width[turn], len(codes))
        lines = []
        for row in range(row_count):
            for col in range(group_count):
                line = []
                self.send_at = {}
                for turn in self.turns:
                    held, codes = sends.get((row, col, turn), (-1, []))
                    self.send_at[turn] = len(line)
                    line += [held] + codes + [-1] * (self.width[turn] - len(codes))
                self.find_at = {}
                for turn in self.turns:
                    for pair in range(PAIR):
                        self.find_at[turn, pair] = len(line)
                        line += [finds.get((row, col, slot, turn, pair), -1) for slot in range(SLOTS)]
                lines.append(line)
        self.table = np.asarray(lines, np.int32)

    def ways(self, row, first, offset, target, group_count):
        both = (first, first + 1)
        if (target % group_count) // PAIR != (row % group_count) // PAIR:
            side = int(abs(offset) == 2)
            return [(int(offset < 0), first + target % PAIR, first + side, both)]
        behind = int(offset < 0)
        sender = first + (target + 1 - behind) % PAIR
        if (target % group_count) // PAIR == first // PAIR:
            return [(2, sender, first + behind, both)]
        return [(2 + (side ^ behind), sender, first + side, (first + side,)) for side in range(PAIR)]

    def blocks(self, row, first, target, row_count, group_count):
        found = []
        for column in range(first, first + PAIR):
            mine = (column - row) % group_count
            theirs = (column - target) % group_count
            have = {(row + mine) % row_count: 0}
            if mine:
                have[(row + mine - group_count) % row_count] = 1
            for slot in range(SLOTS if theirs else 1):
                wanted = (target + theirs - group_count * slot) % row_count
                if wanted in have:
                    found.append((column, slot, have[wanted]))
        return found


def same_pair(group_count):
    pair = (lax.axis_index("row") % group_count) // PAIR
    return (pair == lax.axis_index("col") // PAIR).astype(jnp.int32)


def pack_kernel(group_count, energy, state, *outs):
    rows, _, slots, parts, size, _ = energy.shape
    crossing = same_pair(group_count)
    for row in range(rows):
        for part in range(parts):
            here = pl.ds(part * size, size)
            there = pl.ds((parts + part) * size, size)
            outs[slots][row, here] = energy[row, 0, crossing, part]
            outs[slots][row, there] = state[row, 0, crossing, part].astype(jnp.bfloat16)
    for slot in range(slots):
        for row in range(rows):
            for part in range(parts):
                outs[slot][row, part * size:(part + 1) * size] = energy[row, 0, slot, part]
                outs[slot][row, (parts + part) * size:(parts + part + 1) * size] = state[
                    row, 0, slot, part
                ].astype(jnp.bfloat16)


def fill_right(right, row, place, stack, size):
    energy_re = stack[0 * size:1 * size]
    energy_im = stack[1 * size:2 * size]
    state_re = stack[2 * size:3 * size]
    state_im = stack[3 * size:4 * size]
    right[row, place, 0 * size:1 * size, :size] = state_re
    right[row, place, 0 * size:1 * size, size:] = state_im
    right[row, place, 1 * size:2 * size, :size] = state_im
    right[row, place, 1 * size:2 * size, size:] = -state_re
    right[row, place, 2 * size:3 * size, :size] = -energy_re
    right[row, place, 2 * size:3 * size, size:] = -energy_im
    right[row, place, 3 * size:4 * size, :size] = -energy_im
    right[row, place, 3 * size:4 * size, size:] = energy_re


def times(left, right):
    return lax.dot_general(
        left, right, (((0,), (0,)), ((), ())), preferred_element_type=jnp.float32
    )


def terms_kernel(plan, turns, held_codes, rows, size, line, own_cols, near_cols, *refs):
    columns = refs[:PAIR * SLOTS]
    targets = refs[PAIR * SLOTS:PAIR * SLOTS + len(held_codes)]
    outs, right = refs[-len(turns) - 1:-1], refs[-1]
    for row in range(rows):
        for code in range(PAIR * SLOTS):
            fill_right(right, row, code, columns[code][row], size)
    for row in range(rows):
        held = line[plan.send_at[turns[0]]]
        left = targets[0][row]
        for code, ref in zip(held_codes[1:], targets[1:]):
            left = jnp.where(held == code, ref[row], left)
        for turn, out in zip(turns, outs):
            for place in range(plan.width[turn]):
                code = jnp.maximum(line[plan.send_at[turn] + 1 + place], 0)
                pair = code // SLOTS
                slot = code % SLOTS
                full = times(left, right[row, code]).astype(jnp.bfloat16)
                there = jnp.where(pair == 0, own_cols[row, slot], near_cols[row, slot]) % rows
                out[place, there, 0] = full[:, :size]
                out[place, there, 1] = full[:, size:]


def own_kernel(group_count, rows, size, places, line, own_cols, *refs):
    firsts = refs[SLOTS:SLOTS + group_count]
    early = refs[SLOTS + group_count:-2]
    out, right = refs[-2:]
    me = lax.axis_index("row")
    col = lax.axis_index("col")
    for row in range(rows):
        for slot in range(SLOTS):
            fill_right(right, row, slot, refs[slot][row], size)
    held = (me % group_count) ^ col
    for row in range(rows):
        left = firsts[0][row]
        for place in range(1, group_count):
            left = jnp.where(held == place, firsts[place][row], left)
        for slot in range(SLOTS):
            full = times(left, right[row, slot])
            out[row, slot, 0] = full[:, :size]
            out[row, slot, 1] = full[:, size:]

    @pl.when(held == 0)
    def _():
        for row in range(rows):
            partner = own_cols[row, 1] % rows
            for slot in range(SLOTS):
                full = times(refs[1][partner], right[partner, 1 - slot])
                out[row, slot, 0] += full[:, :size]
                out[row, slot, 1] += full[:, size:]

    for row in range(rows):
        for slot in range(SLOTS):
            out[row, slot] = add_terms(out[row, slot], row, slot, places, line, own_cols, early)


def add_terms(total, row, slot, places, line, cols, terms):
    for place, ref in zip(places, terms):
        found = line[place + slot]
        block = ref[jnp.maximum(found, 0), cols[row, slot] % cols.shape[0]]
        total += jnp.where(found >= 0, block, 0.0).astype(jnp.float32)
    return total


def finish_kernel(places, line, cols, own, density, *refs):
    terms = refs[:len(places)]
    commutator, section = refs[len(places):]
    rows, slots = own.shape[:2]
    for row in range(rows):
        for slot in range(slots):
            total = add_terms(own[row, slot], row, slot, places, line, cols, terms)
            commutator[row, 0, slot] = total
            section[row, 0, slot, 0] = density[row, 0, slot, 0] + 0.05 * total[1]
            section[row, 0, slot, 1] = density[row, 0, slot, 1] - 0.05 * total[0]


def body(plan, hamiltonian, density, block_cols):
    group_count = lax.axis_size("col")
    rows, _, slots, parts, size, _ = hamiltonian.shape
    smem = pl.BlockSpec(memory_space=pltpu.SMEM)
    vmem = pl.BlockSpec(memory_space=pltpu.VMEM)
    params = pltpu.CompilerParams(vmem_limit_bytes=40 * 1024 * 1024)

    device = lax.axis_index("row") * group_count + lax.axis_index("col")
    line = lax.dynamic_index_in_dim(jnp.asarray(plan.table), device, 0, keepdims=False)
    own_cols = block_cols[:, 0]
    own_0, own_1, first_out = pl.pallas_call(
        functools.partial(pack_kernel, group_count),
        out_shape=[jax.ShapeDtypeStruct((rows, 2 * parts * size, size), jnp.bfloat16)] * 3,
        in_specs=[vmem] * 2,
        out_specs=[vmem] * 3,
        compiler_params=params,
        name="pack",
    )(hamiltonian, density)
    first_in = xor_col(first_out, group_count, PAIR)
    near_0 = xor_col(own_0, group_count, 1)
    near_1 = xor_col(own_1, group_count, 1)
    second_out = jnp.where(same_pair(group_count) == 1, near_0, own_1)
    second_in = xor_col(second_out, group_count, PAIR)
    columns = [own_0, own_1, near_0, near_1]
    near_cols = xor_col(own_cols, group_count, 1)

    arrived = {}

    def send(turns, held):
        sent = pl.pallas_call(
            functools.partial(terms_kernel, plan, turns, list(held), rows, size),
            out_shape=[
                jax.ShapeDtypeStruct((plan.width[turn], rows, parts, size, size), jnp.bfloat16)
                for turn in turns
            ],
            in_specs=[smem, smem, smem] + [vmem] * (len(columns) + len(held)),
            out_specs=[vmem] * len(turns),
            scratch_shapes=[pltpu.VMEM((rows, PAIR * SLOTS, 4 * size, 2 * size), jnp.bfloat16)],
            compiler_params=params,
            cost_estimate=pl.CostEstimate(flops=20000000, bytes_accessed=60000, transcendentals=0),
            name="terms_%d" % turns[0],
        )(line, own_cols, near_cols, *columns, *held.values())
        for turn, one in zip(turns, sent):
            arrived[turn] = lax.ppermute(one, ("row", "col"), plan.pairs[turn])
        return sent

    send([0], {0: own_0, 4: first_in})
    send([1], {1: own_1, 5: second_in})
    sent = send([2, 3], {1: own_1, 2: near_0, 5: first_in, 6: second_in})[0]
    late, _ = lax.optimization_barrier((second_in, sent))
    late = xor_col(late, group_count, 1)

    swapped = {0: xor_col(arrived[0], group_count, 1)}
    early = [arrived[0], swapped[0]]
    places = [plan.find_at[0, 0], plan.find_at[0, 1]]
    own = pl.pallas_call(
        functools.partial(own_kernel, group_count, rows, size, places),
        out_shape=jax.ShapeDtypeStruct((rows, slots, parts, size, size), jnp.float32),
        in_specs=[smem, smem] + [vmem] * (SLOTS + group_count + len(early)),
        out_specs=vmem,
        scratch_shapes=[pltpu.VMEM((rows, SLOTS, 4 * size, 2 * size), jnp.bfloat16)],
        compiler_params=params,
        cost_estimate=pl.CostEstimate(flops=20000000, bytes_accessed=60000, transcendentals=0),
            name="own_terms",
    )(line, own_cols, own_0, own_1, own_0, near_0, late, second_in, *early)

    arrived[1], arrived[3] = lax.optimization_barrier((arrived[1], arrived[3]))
    swapped[1] = xor_col(arrived[1], group_count, 1)
    swapped[2] = xor_col(arrived[2], group_count, 1)
    terms = [arrived[1], arrived[2], arrived[3], swapped[1], swapped[2]]
    places = [plan.find_at[turn, 0] for turn in (1, 2, 3)] + [plan.find_at[turn, 1] for turn in (1, 2)]

    commutator, section = pl.pallas_call(
        functools.partial(finish_kernel, places),
        out_shape=[jax.ShapeDtypeStruct(density.shape, jnp.float32)] * 2,
        in_specs=[smem] * 2 + [vmem] * (2 + len(terms)),
        out_specs=[vmem] * 2,
        compiler_params=params,
        name="finish",
    )(line, own_cols, own, density, *terms)
    return commutator, section


def solution(mesh):
    plan = Plan(mesh.shape["row"], mesh.shape["col"])
    blocks = P("row", "col", None, None, None, None)
    return jax.shard_map(
        functools.partial(body, plan),
        mesh=mesh,
        in_specs=(blocks, blocks, P("row", "col", None)),
        out_specs=(blocks, blocks),
        check_vma=False,
    )
```
